1024 devices in a mesh: gx: 16 (over x_lo, y), gy: 64 (over x_hi, z, core).
Axes of the slice: x: 8 (x_hi: 4, x_lo: 2; x = x_hi * 2 + x_lo), y: 8, z: 8, core: 2. Of those that a mesh axis runs over, the one named last changes fastest.
Arguments:
- tokens: bfloat16 [1024, 18432], P('gy', 'gx'), may hold values from -6 to 6
- qkv_weight: bfloat16 [18432, 12800], P('gx', 'gy'), may hold values from -0.046875 to 0.046875
- out_weight: bfloat16 [12288, 18432], P(None, 'gy'), may hold values from -1.25 to 1.25
- cache: bfloat16 [1024, 2, 2048, 256], P(('gx', 'gy')), may hold values from -2000 to 2000
- cache_lengths: int32 [1024], P(('gx', 'gy')), may hold values from 16 to 2048, as said below
Outputs:
- mixed: bfloat16 [1024, 18432], P('gx', 'gy')
The draws below stay inside these ranges and needn't reach their ends.
Inputs may be any that keep to these rules, and one draw needn't show every extreme that they name: `cache_lengths`: at least one sequence has exactly 2048 valid slots; lengths are spread from 16 to 2048 in scale.
All inputs are finite; a program needn't handle non-finite values.
Results may differ from the reference program's by a relative error of at most 0.01.
The reference program's roundings to bfloat16 on the way count: a program that leaves them out, or rounds other values in their place, can miss the bound.
Values may be sent and summed in bfloat16 or wider, within the bound.
No kernel may reach another device: no remote copies, remote signals or barrier semaphores. Data moves between devices by JAX's collectives and lax.ppermute only.
A program may use at most 32 MiB of HBM per device.

```python
import jax
import jax.numpy as jnp
from jax import lax

D = 18432
HEADS = 48
DH = 256
L = 2048
HD = 12288
QKV = 12800
SEQS = 1024


def draw_cache(key, part):
    key = jax.random.fold_in(key, 11)
    shape = (SEQS, 2, L, DH)
    base = jnp.clip(jax.random.normal(key, shape, jnp.float32), -4.0, 4.0)
    return base.astype(jnp.bfloat16)


def draw_cache_lengths(key, part):
    key = jax.random.fold_in(key, 23)
    top = L.bit_length() - 1
    expo = jax.random.randint(jax.random.fold_in(key, 1), (SEQS,), 4, top + 1)
    lowest = jnp.left_shift(jnp.ones((SEQS,), jnp.int32), expo)
    extra = jax.random.randint(jax.random.fold_in(key, 2), (SEQS,), 0, lowest)
    length = jnp.minimum(lowest + extra, L)
    chosen = jax.random.randint(jax.random.fold_in(key, 3), (), 0, SEQS)
    length = jnp.where(jnp.arange(SEQS) == chosen, L, length)
    return length.astype(jnp.int32)


def steps_of(key, extent, pieces, low, largest):
    factor_of, own = 1.0, jax.random.fold_in(key, 6)
    for axis_at, blocks in pieces:
        draws = jnp.exp(jax.random.uniform(jax.random.fold_in(own, axis_at), (blocks,), jnp.float32, low / len(pieces), largest / len(pieces)))
        factor_of = factor_of * jnp.repeat(draws, extent[axis_at] // blocks).reshape([-1 if axis == axis_at else 1 for axis in range(len(extent))])
    return factor_of


def gaussian(key, shape, width, reach, cuts=(), held_as=jnp.bfloat16):
    level = steps_of(key, shape, cuts, -0.22, 0.18) if cuts else 1.0
    values = jax.random.normal(key, shape, jnp.float32) * width * level
    return jnp.minimum(jnp.maximum(values, -reach), reach).astype(held_as)


def setup_inputs(seed: int = 0) -> dict:
    splits = jax.random.split(jax.random.key(seed), 6)
    return {
        "tokens": gaussian(splits[0], (SEQS, D), 1.0, 6.0, ((0, 64), (1, 16))),
        "qkv_weight": gaussian(splits[1], (D, QKV), D ** -0.5, 0.046875, ((0, 16), (1, 64))),
        "out_weight": gaussian(splits[2], (HD, D), (max(HD // 512, 1)) ** -0.5, 1.25, ((1, 64),)),
        "cache": draw_cache(jax.random.fold_in(splits[5], 71), 0),
        "cache_lengths": draw_cache_lengths(jax.random.fold_in(splits[5], 71), 0),
    }


def rotate(vectors, token_position):
    half = vectors.shape[-1] // 2
    steps = jnp.arange(half).astype(jnp.float32)
    freqs = 10000.0 ** (-2.0 * steps / vectors.shape[-1])
    angle = token_position * freqs
    cosine = jnp.cos(angle)
    sine = jnp.sin(angle)
    first = vectors[..., :half]
    second = vectors[..., half:]
    return jnp.concatenate([first * cosine - second * sine, second * cosine + first * sine], axis=-1)


def attend_one(items):
    query_vector, fresh_key, fresh_value, block, length = items
    score_scale = DH ** -0.5
    keys = block[0].astype(jnp.float32)
    values = block[1].astype(jnp.float32)
    query32 = query_vector.astype(jnp.float32)
    scores = jnp.einsum("hd,ld->hl", query32, keys) * score_scale
    valid = jnp.arange(L).astype(jnp.int32) < length
    scores = jnp.where(valid[None, :], scores, -1e30)
    fresh = jnp.einsum("hd,d->h", query32, fresh_key.astype(jnp.float32)) * score_scale
    top = jnp.maximum(jnp.max(scores, axis=-1), fresh)
    expo = jnp.exp(scores - top[:, None])
    expo_fresh = jnp.exp(fresh - top)
    total = jnp.sum(expo, axis=-1) + expo_fresh
    softmax_weights = (expo / total[:, None]).astype(jnp.bfloat16)
    fresh_weight = (expo_fresh / total).astype(jnp.bfloat16)
    attended_output = jnp.einsum("hl,ld->hd", softmax_weights.astype(jnp.float32), values)
    attended_output = attended_output + fresh_weight.astype(jnp.float32)[:, None] * fresh_value.astype(jnp.float32)[None, :]
    return attended_output.astype(jnp.bfloat16)


def reference(tokens, qkv_weight, out_weight, cache, cache_lengths):
    proj = jnp.dot(tokens, qkv_weight, preferred_element_type=jnp.float32).astype(jnp.bfloat16)
    token_position = cache_lengths.astype(jnp.float32)
    query_vector = proj[:, :HD].astype(jnp.float32).reshape(SEQS, HEADS, DH)
    query_vector = rotate(query_vector, token_position[:, None, None]).astype(jnp.bfloat16)
    fresh_key = rotate(proj[:, HD:HD + DH].astype(jnp.float32), token_position[:, None]).astype(jnp.bfloat16)
    fresh_value = proj[:, HD + DH:]
    attended_output = lax.map(attend_one, (query_vector, fresh_key, fresh_value, cache, cache_lengths))
    attended_output = attended_output.reshape(SEQS, HD)
    return jnp.dot(attended_output, out_weight, preferred_element_type=jnp.float32).astype(jnp.bfloat16)
```

```python
import jax
import jax.numpy as jnp
from jax import lax
from jax.sharding import PartitionSpec as P

HEADS = 48
DH = 256

CHIPS = 32
PLANE = [[2 * chip + core for chip in range(CHIPS)] for core in range(2)]
SIBLING = [(i, i ^ 1) for i in range(2 * CHIPS)]


def rotate(vectors, token_position):
    half = vectors.shape[-1] // 2
    steps = jnp.arange(half).astype(jnp.float32)
    freqs = 10000.0 ** (-2.0 * steps / vectors.shape[-1])
    angle = token_position * freqs
    cosine = jnp.cos(angle)
    sine = jnp.sin(angle)
    first = vectors[..., :half]
    second = vectors[..., half:]
    return jnp.concatenate(
        [first * cosine - second * sine, second * cosine + first * sine], axis=-1
    )


def attend_cached_keys(proj, cache, cache_lengths):
    seq_here = proj.shape[0]
    width = HEADS * DH
    score_scale = DH ** (-0.5)
    token_position = cache_lengths.astype(jnp.float32)
    query_vector = proj[:, :width].astype(jnp.float32).reshape(seq_here, HEADS, DH)
    query_vector = rotate(query_vector, token_position[:, None, None]).astype(jnp.bfloat16)
    fresh_key = rotate(
        proj[:, width : width + DH].astype(jnp.float32), token_position[:, None]
    ).astype(jnp.bfloat16)
    fresh_value = proj[:, width + DH :]
    scores = (
        jnp.einsum("bpr,bar->bpa", query_vector, cache[:, 0], preferred_element_type=jnp.float32)
        * score_scale
    )
    valid = jnp.arange(cache.shape[2])[None, :] < cache_lengths[:, None]
    scores = jnp.where(valid[:, None, :], scores, -1e30)
    fresh = (
        jnp.einsum("shd,sd->sh", query_vector, fresh_key, preferred_element_type=jnp.float32)
        * score_scale
    )
    top = jnp.maximum(jnp.max(scores, axis=-1), fresh)
    expo = jnp.exp(scores - top[:, :, None])
    expo_fresh = jnp.exp(fresh - top)
    total = jnp.sum(expo, axis=-1) + expo_fresh
    softmax_weights = (expo / total[:, :, None]).astype(jnp.bfloat16)
    fresh_weight = (expo_fresh / total).astype(jnp.bfloat16)
    attended_output = jnp.einsum(
        "trj,tjp->trp", softmax_weights, cache[:, 1], preferred_element_type=jnp.float32
    )
    attended_output = (
        attended_output
        + fresh_weight.astype(jnp.float32)[:, :, None] * fresh_value.astype(jnp.float32)[:, None, :]
    )
    return attended_output.astype(jnp.bfloat16)


def over_plane(blocks):
    return lax.all_to_all(
        blocks, "gy", split_axis=0, concat_axis=0, axis_index_groups=PLANE, tiled=True
    )


def on_device(tokens, qkv_weight, out_weight, cache, cache_lengths):
    core = lax.rem(lax.axis_index("gy"), 2)
    other_weight = lax.ppermute(qkv_weight, "gy", SIBLING)
    pairs = tokens.reshape(8, 2, -1)
    even, odd = pairs[:, 0], pairs[:, 1]
    kept = jnp.where(core == 0, even, odd)
    given = jnp.where(core == 0, odd, even)
    taken = lax.ppermute(given, "gy", SIBLING)
    rows = jnp.where(
        core == 0,
        jnp.concatenate([kept, taken], axis=0),
        jnp.concatenate([taken, kept], axis=0),
    )
    gathered = over_plane(jnp.broadcast_to(rows[None], (CHIPS,) + rows.shape))
    gathered = gathered.reshape(CHIPS * 16, -1)
    weights = jnp.concatenate([qkv_weight, other_weight], axis=1)
    partial_value = jnp.dot(gathered, weights, preferred_element_type=jnp.float32)
    parts = lax.all_to_all(
        partial_value.reshape(16, 32, -1), "gx", split_axis=0, concat_axis=0, tiled=True
    )
    summed = jnp.sum(parts, axis=0)
    columns = summed.shape[1] // 2
    summed = jnp.where(core == 0, summed, jnp.roll(summed, columns, axis=1)).astype(jnp.bfloat16)
    proj = over_plane(summed).reshape(1, -1)
    attended_output = attend_cached_keys(proj, cache, cache_lengths).reshape(1, 96, 128)
    mine = over_plane(jnp.broadcast_to(attended_output, (CHIPS, 96, 128)))
    theirs = lax.ppermute(mine, "gy", SIBLING)
    both = jnp.concatenate([mine, theirs], axis=0).reshape(2 * CHIPS, -1)
    mixed = jnp.dot(both, out_weight, preferred_element_type=jnp.float32).astype(jnp.bfloat16)
    mixed = mixed.reshape(2, CHIPS, -1)
    mixed = jnp.where(core == 0, mixed, mixed[::-1])
    return mixed.transpose(1, 0, 2).reshape(2 * CHIPS, -1)


def solution(mesh):
    placed = (
        P("gy", "gx"),
        P("gx", "gy"),
        P(None, "gy"),
        P(("gx", "gy"), None, None, None),
        P(("gx", "gy")),
    )
    return jax.shard_map(
        on_device, mesh=mesh, in_specs=placed, out_specs=P("gx", "gy"), check_vma=False
    )
```

```python
import jax
import jax.numpy as jnp
from jax import lax
from jax.sharding import PartitionSpec as P

HEADS = 48
DH = 256

CHIPS = 32
PLANE = [[2 * chip + core for chip in range(CHIPS)] for core in range(2)]
SIBLING = [(i, i ^ 1) for i in range(2 * CHIPS)]
NEXT_PLANE = [(i, i ^ 1) for i in range(16)]


def rotate(vectors, token_position):
    half = vectors.shape[-1] // 2
    steps = jnp.arange(half).astype(jnp.float32)
    freqs = 10000.0 ** (-2.0 * steps / vectors.shape[-1])
    angle = token_position * freqs
    cosine = jnp.cos(angle)
    sine = jnp.sin(angle)
    first = vectors[..., :half]
    second = vectors[..., half:]
    return jnp.concatenate(
        [first * cosine - second * sine, second * cosine + first * sine], axis=-1
    )


def attend_cached_keys(proj, cache, cache_lengths):
    seq_here = proj.shape[0]
    width = HEADS * DH
    score_scale = DH ** (-0.5)
    token_position = cache_lengths.astype(jnp.float32)
    query_vector = proj[:, :width].astype(jnp.float32).reshape(seq_here, HEADS, DH)
    query_vector = rotate(query_vector, token_position[:, None, None]).astype(jnp.bfloat16)
    fresh_key = rotate(
        proj[:, width : width + DH].astype(jnp.float32), token_position[:, None]
    ).astype(jnp.bfloat16)
    fresh_value = proj[:, width + DH :]
    scores = (
        jnp.einsum("bpr,bar->bpa", query_vector, cache[:, 0], preferred_element_type=jnp.float32)
        * score_scale
    )
    valid = jnp.arange(cache.shape[2])[None, :] < cache_lengths[:, None]
    scores = jnp.where(valid[:, None, :], scores, -1e30)
    fresh = (
        jnp.einsum("shd,sd->sh", query_vector, fresh_key, preferred_element_type=jnp.float32)
        * score_scale
    )
    top = jnp.maximum(jnp.max(scores, axis=-1), fresh)
    expo = jnp.exp(scores - top[:, :, None])
    expo_fresh = jnp.exp(fresh - top)
    total = jnp.sum(expo, axis=-1) + expo_fresh
    softmax_weights = (expo / total[:, :, None]).astype(jnp.bfloat16)
    fresh_weight = (expo_fresh / total).astype(jnp.bfloat16)
    attended_output = jnp.einsum(
        "trj,tjp->trp", softmax_weights, cache[:, 1], preferred_element_type=jnp.float32
    )
    attended_output = (
        attended_output
        + fresh_weight.astype(jnp.float32)[:, :, None] * fresh_value.astype(jnp.float32)[:, None, :]
    )
    return attended_output.astype(jnp.bfloat16)


def over_plane(blocks):
    return lax.all_to_all(
        blocks, "gy", split_axis=0, concat_axis=0, axis_index_groups=PLANE, tiled=True
    )


def swap_rows(rows, mine, axis, pairs):
    split = rows.reshape((rows.shape[0] // 2, 2) + rows.shape[1:])
    even, odd = split[:, 0], split[:, 1]
    kept = jnp.where(mine == 0, even, odd)
    return kept, lax.ppermute(jnp.where(mine == 0, odd, even), axis, pairs)


def on_device(tokens, qkv_weight, out_weight, cache, cache_lengths):
    core = lax.rem(lax.axis_index("gy"), 2)
    plane = lax.rem(lax.axis_index("gx"), 2)
    kept, taken = swap_rows(tokens, core, "gy", SIBLING)
    rows = jnp.where(
        core == 0,
        jnp.concatenate([kept, taken], axis=0),
        jnp.concatenate([taken, kept], axis=0),
    )
    rows = jnp.concatenate(swap_rows(rows, plane, "gx", NEXT_PLANE), axis=1)
    next_weight = lax.ppermute(qkv_weight, "gx", NEXT_PLANE)
    own_columns = jnp.concatenate([qkv_weight, next_weight], axis=0)
    weights = jnp.concatenate([own_columns, lax.ppermute(own_columns, "gy", SIBLING)], axis=1)
    gathered = over_plane(jnp.broadcast_to(rows[None], (CHIPS,) + rows.shape))
    partial_value = jnp.dot(
        gathered.reshape(CHIPS * 8, -1), weights, preferred_element_type=jnp.float32
    )
    parts = lax.all_to_all(
        partial_value.reshape(16, 16, -1), "gx", split_axis=0, concat_axis=0, tiled=True
    )
    summed = jnp.sum(parts.reshape((8, 2) + parts.shape[1:]), axis=0)
    summed = summed.transpose(1, 0, 2).reshape(CHIPS, -1)
    columns = summed.shape[1] // 2
    summed = jnp.where(core == 0, summed, jnp.roll(summed, columns, axis=1)).astype(jnp.bfloat16)
    proj = over_plane(summed).reshape(1, -1)
    attended_output = attend_cached_keys(proj, cache, cache_lengths).reshape(1, 96, 128)
    mine = over_plane(jnp.broadcast_to(attended_output, (CHIPS, 96, 128)))
    theirs = lax.ppermute(mine, "gy", SIBLING)
    both = jnp.concatenate([mine, theirs], axis=0).reshape(2 * CHIPS, -1)
    mixed = jnp.dot(both, out_weight, preferred_element_type=jnp.float32).astype(jnp.bfloat16)
    mixed = mixed.reshape(2, CHIPS, -1)
    mixed = jnp.where(core == 0, mixed, mixed[::-1])
    return mixed.transpose(1, 0, 2).reshape(2 * CHIPS, -1)


def solution(mesh):
    placed = (
        P("gy", "gx"),
        P("gx", "gy"),
        P(None, "gy"),
        P(("gx", "gy"), None, None, None),
        P(("gx", "gy")),
    )
    return jax.shard_map(
        on_device, mesh=mesh, in_specs=placed, out_specs=P("gx", "gy"), check_vma=False
    )
```

```python
import jax
import jax.numpy as jnp
from jax import lax
from jax.sharding import PartitionSpec as P

HEADS = 48
DH = 256

CHIPS = 32


def place(x_hi, z, core):
    return (x_hi * 8 + z) * 2 + core


def near_group(core, x_from, z_from):
    members = {}
    for dx in range(2):
        for dz in range(2):
            x_hi, z = (x_from + dx) % 4, (z_from + dz) % 8
            members[x_hi % 2, z % 2] = place(x_hi, z, core)
    return [members[key] for key in sorted(members)]


PLANE = [[place(chip // 8, chip % 8, core) for chip in range(CHIPS)] for core in range(2)]
NEAR = [
    near_group(core, 2 * a + core, 2 * b + core)
    for core in range(2)
    for a in range(2)
    for b in range(4)
]
FAR = [
    [
        (2 * pair + plane) * 64 + place(2 * a + e, 2 * b + w, core)
        for plane in range(2)
        for a in range(2)
        for b in range(4)
        for core in range(2)
    ]
    for pair in range(8)
    for e in range(2)
    for w in range(2)
]
SIBLING = [(i, i ^ 1) for i in range(2 * CHIPS)]
NEXT_PLANE = [(i, i ^ 1) for i in range(16)]


def rotate(vectors, token_position):
    half = vectors.shape[-1] // 2
    steps = jnp.arange(half).astype(jnp.float32)
    freqs = 10000.0 ** (-2.0 * steps / vectors.shape[-1])
    angle = token_position * freqs
    cosine = jnp.cos(angle)
    sine = jnp.sin(angle)
    first = vectors[..., :half]
    second = vectors[..., half:]
    return jnp.concatenate(
        [first * cosine - second * sine, second * cosine + first * sine], axis=-1
    )


def attend_cached_keys(proj, cache, cache_lengths):
    seq_here = proj.shape[0]
    width = HEADS * DH
    score_scale = DH ** (-0.5)
    token_position = cache_lengths.astype(jnp.float32)
    query_vector = proj[:, :width].astype(jnp.float32).reshape(seq_here, HEADS, DH)
    query_vector = rotate(query_vector, token_position[:, None, None]).astype(jnp.bfloat16)
    fresh_key = rotate(
        proj[:, width : width + DH].astype(jnp.float32), token_position[:, None]
    ).astype(jnp.bfloat16)
    fresh_value = proj[:, width + DH :]
    scores = (
        jnp.einsum("bpr,bar->bpa", query_vector, cache[:, 0], preferred_element_type=jnp.float32)
        * score_scale
    )
    valid = jnp.arange(cache.shape[2])[None, :] < cache_lengths[:, None]
    scores = jnp.where(valid[:, None, :], scores, -1e30)
    fresh = (
        jnp.einsum("shd,sd->sh", query_vector, fresh_key, preferred_element_type=jnp.float32)
        * score_scale
    )
    top = jnp.maximum(jnp.max(scores, axis=-1), fresh)
    expo = jnp.exp(scores - top[:, :, None])
    expo_fresh = jnp.exp(fresh - top)
    total = jnp.sum(expo, axis=-1) + expo_fresh
    softmax_weights = (expo / total[:, :, None]).astype(jnp.bfloat16)
    fresh_weight = (expo_fresh / total).astype(jnp.bfloat16)
    attended_output = jnp.einsum(
        "trj,tjp->trp", softmax_weights, cache[:, 1], preferred_element_type=jnp.float32
    )
    attended_output = (
        attended_output
        + fresh_weight.astype(jnp.float32)[:, :, None] * fresh_value.astype(jnp.float32)[:, None, :]
    )
    return attended_output.astype(jnp.bfloat16)


def exchange(blocks, axis, groups):
    return lax.all_to_all(
        blocks, axis, split_axis=0, concat_axis=0, axis_index_groups=groups, tiled=True
    )


def on_device(tokens, qkv_weight, out_weight, cache, cache_lengths):
    core = lax.rem(lax.axis_index("gy"), 2)
    plane = lax.rem(lax.axis_index("gx"), 2)
    width = tokens.shape[1]
    split = tokens.reshape(4, 2, 2, width).transpose(1, 2, 0, 3)
    far = jnp.broadcast_to(split[:, None], (2, 8, 2, 4, width)).reshape(CHIPS, 4, width)
    far = exchange(far, ("gx", "gy"), FAR).reshape(2, 64, width)
    rows = jnp.concatenate([far[0], far[1]], axis=1)
    gathered = exchange(jnp.broadcast_to(rows[None], (4,) + rows.shape), "gy", NEAR)
    next_weight = lax.ppermute(qkv_weight, "gx", NEXT_PLANE)
    own_columns = jnp.concatenate(
        [
            jnp.where(plane == 0, qkv_weight, next_weight),
            jnp.where(plane == 0, next_weight, qkv_weight),
        ],
        axis=0,
    )
    weights = jnp.concatenate([own_columns, lax.ppermute(own_columns, "gy", SIBLING)], axis=1)
    partial_value = jnp.dot(
        gathered.reshape(256, 2 * width), weights, preferred_element_type=jnp.float32
    )
    columns = partial_value.shape[1]
    partial_value = partial_value.reshape(2, 2, 2, 4, 8, columns).transpose(2, 0, 3, 1, 4, 5)
    parts = exchange(partial_value.reshape(16, 16, columns), "gx", None)
    summed = jnp.sum(parts.reshape(8, 2, 16, columns), axis=0)
    summed = summed.transpose(1, 0, 2).reshape(CHIPS, columns)
    summed = jnp.where(core == 0, summed, jnp.roll(summed, columns // 2, axis=1))
    summed = jnp.pad(summed.astype(jnp.bfloat16), ((0, 0), (0, 512 - columns)))
    proj = exchange(summed.reshape(CHIPS, 4, 128), "gy", PLANE).reshape(CHIPS, 512)
    proj = proj[:, :columns].reshape(1, -1)
    attended_output = attend_cached_keys(proj, cache, cache_lengths).reshape(1, 96, 128)
    mine = exchange(jnp.broadcast_to(attended_output, (CHIPS, 96, 128)), "gy", PLANE)
    theirs = lax.ppermute(mine, "gy", SIBLING)
    both = jnp.concatenate([mine, theirs], axis=0).reshape(2 * CHIPS, -1)
    mixed = jnp.dot(both, out_weight, preferred_element_type=jnp.float32).astype(jnp.bfloat16)
    mixed = mixed.reshape(2, CHIPS, -1)
    mixed = jnp.where(core == 0, mixed, mixed[::-1])
    return mixed.transpose(1, 0, 2).reshape(2 * CHIPS, -1)


def solution(mesh):
    placed = (
        P("gy", "gx"),
        P("gx", "gy"),
        P(None, "gy"),
        P(("gx", "gy"), None, None, None),
        P(("gx", "gy")),
    )
    return jax.shard_map(
        on_device, mesh=mesh, in_specs=placed, out_specs=P("gx", "gy"), check_vma=False
    )
```

```python
import jax
import jax.numpy as jnp
from jax import lax
from jax.experimental import pallas as pl
from jax.experimental.pallas import tpu as pltpu
from jax.sharding import PartitionSpec as P

HEADS = 48
DH = 256

CHIPS = 32


def place(x_hi, z, core):
    return (x_hi * 8 + z) * 2 + core


def near_group(core, x_from, z_from):
    members = {}
    for dx in range(2):
        for dz in range(2):
            x_hi, z = (x_from + dx) % 4, (z_from + dz) % 8
            members[x_hi % 2, z % 2] = place(x_hi, z, core)
    return [members[key] for key in sorted(members)]


PLANE = [[place(chip // 8, chip % 8, core) for chip in range(CHIPS)] for core in range(2)]
NEAR = [
    near_group(core, 2 * a + core, 2 * b + core)
    for core in range(2)
    for a in range(2)
    for b in range(4)
]
FAR = [
    [
        (2 * pair + plane) * 64 + place(2 * a + e, 2 * b + w, core)
        for plane in range(2)
        for a in range(2)
        for b in range(4)
        for core in range(2)
    ]
    for pair in range(8)
    for e in range(2)
    for w in range(2)
]
SIBLING = [(i, i ^ 1) for i in range(2 * CHIPS)]
NEXT_PLANE = [(i, i ^ 1) for i in range(16)]


def rotate(vectors, token_position):
    half = vectors.shape[-1] // 2
    steps = jnp.arange(half).astype(jnp.float32)
    freqs = 10000.0 ** (-2.0 * steps / vectors.shape[-1])
    angle = token_position * freqs
    cosine = jnp.cos(angle)
    sine = jnp.sin(angle)
    first = vectors[..., :half]
    second = vectors[..., half:]
    return jnp.concatenate(
        [first * cosine - second * sine, second * cosine + first * sine], axis=-1
    )


def attend_cached_keys(proj, cache, cache_lengths):
    seq_here = proj.shape[0]
    width = HEADS * DH
    score_scale = DH ** (-0.5)
    token_position = cache_lengths.astype(jnp.float32)
    query_vector = proj[:, :width].astype(jnp.float32).reshape(seq_here, HEADS, DH)
    query_vector = rotate(query_vector, token_position[:, None, None]).astype(jnp.bfloat16)
    fresh_key = rotate(
        proj[:, width : width + DH].astype(jnp.float32), token_position[:, None]
    ).astype(jnp.bfloat16)
    fresh_value = proj[:, width + DH :]
    scores = (
        jnp.einsum("bpr,bar->bpa", query_vector, cache[:, 0], preferred_element_type=jnp.float32)
        * score_scale
    )
    valid = jnp.arange(cache.shape[2])[None, :] < cache_lengths[:, None]
    scores = jnp.where(valid[:, None, :], scores, -1e30)
    fresh = (
        jnp.einsum("shd,sd->sh", query_vector, fresh_key, preferred_element_type=jnp.float32)
        * score_scale
    )
    top = jnp.maximum(jnp.max(scores, axis=-1), fresh)
    expo = jnp.exp(scores - top[:, :, None])
    expo_fresh = jnp.exp(fresh - top)
    total = jnp.sum(expo, axis=-1) + expo_fresh
    softmax_weights = (expo / total[:, :, None]).astype(jnp.bfloat16)
    fresh_weight = (expo_fresh / total).astype(jnp.bfloat16)
    attended_output = jnp.einsum(
        "trj,tjp->trp", softmax_weights, cache[:, 1], preferred_element_type=jnp.float32
    )
    attended_output = (
        attended_output
        + fresh_weight.astype(jnp.float32)[:, :, None] * fresh_value.astype(jnp.float32)[:, None, :]
    )
    return attended_output.astype(jnp.bfloat16)


def exchange(blocks, axis, groups):
    return lax.all_to_all(
        blocks, axis, split_axis=0, concat_axis=0, axis_index_groups=groups, tiled=True
    )


CHUNKS = 6


def output_kernel(core_ref, mine_ref, theirs_ref, weights_ref, out_ref):
    tiles = mine_ref.shape[1] // CHUNKS
    depth = tiles * mine_ref.shape[2]
    total = jnp.zeros((weights_ref.shape[0], 2 * CHIPS), jnp.float32)
    for i in range(CHUNKS):
        here = slice(i * tiles, (i + 1) * tiles)
        rows = jnp.concatenate(
            [
                mine_ref[:, here, :].reshape(CHIPS, depth),
                theirs_ref[:, here, :].reshape(CHIPS, depth),
            ],
            axis=0,
        )
        total += lax.dot_general(
            weights_ref[:, i * depth : (i + 1) * depth],
            rows,
            (((1,), (1,)), ((), ())),
            preferred_element_type=jnp.float32,
        )
    place_of = lax.broadcasted_iota(jnp.int32, (2 * CHIPS, 2 * CHIPS), 0)
    row = lax.broadcasted_iota(jnp.int32, (2 * CHIPS, 2 * CHIPS), 1)
    order = ((place_of >> 1) == (row & (CHIPS - 1))) & (
        (place_of & 1) == ((row >> 5) ^ core_ref[0])
    )
    out_ref[...] = lax.dot_general(
        order.astype(jnp.float32).astype(jnp.bfloat16),
        total.astype(jnp.bfloat16),
        (((1,), (1,)), ((), ())),
        preferred_element_type=jnp.float32,
    ).astype(jnp.bfloat16)


def output_rows(core, mine, theirs, weights):
    columns, depth = weights.shape
    vmem = pl.BlockSpec(memory_space=pltpu.VMEM)
    return pl.pallas_call(
        output_kernel,
        out_shape=jax.ShapeDtypeStruct((2 * CHIPS, columns), jnp.bfloat16),
        in_specs=[pl.BlockSpec(memory_space=pltpu.SMEM), vmem, vmem, vmem],
        out_specs=vmem,
        compiler_params=pltpu.CompilerParams(vmem_limit_bytes=32 * 2**20),
        cost_estimate=pl.CostEstimate(
            flops=4 * CHIPS * columns * depth,
            bytes_accessed=2 * columns * depth,
            transcendentals=0,
        ),
    )(core.astype(jnp.int32).reshape(1), mine, theirs, weights)


def on_device(tokens, qkv_weight, out_weight, cache, cache_lengths):
    core = lax.rem(lax.axis_index("gy"), 2)
    plane = lax.rem(lax.axis_index("gx"), 2)
    width = tokens.shape[1]
    split = tokens.reshape(4, 2, 2, width).transpose(1, 2, 0, 3)
    far = jnp.broadcast_to(split[:, None], (2, 8, 2, 4, width)).reshape(CHIPS, 4, width)
    far = exchange(far, ("gx", "gy"), FAR).reshape(2, 64, width)
    rows = jnp.concatenate([far[0], far[1]], axis=1)
    gathered = exchange(jnp.broadcast_to(rows[None], (4,) + rows.shape), "gy", NEAR)
    next_weight = lax.ppermute(qkv_weight, "gx", NEXT_PLANE)
    own_columns = jnp.concatenate(
        [
            jnp.where(plane == 0, qkv_weight, next_weight),
            jnp.where(plane == 0, next_weight, qkv_weight),
        ],
        axis=0,
    )
    weights = jnp.concatenate([own_columns, lax.ppermute(own_columns, "gy", SIBLING)], axis=1)
    partial_value = jnp.dot(
        gathered.reshape(256, 2 * width), weights, preferred_element_type=jnp.float32
    )
    columns = partial_value.shape[1]
    partial_value = partial_value.reshape(2, 2, 2, 4, 8, columns).transpose(2, 0, 3, 1, 4, 5)
    parts = exchange(partial_value.reshape(16, 16, columns), "gx", None)
    summed = jnp.sum(parts.reshape(8, 2, 16, columns), axis=0)
    summed = summed.transpose(1, 0, 2).reshape(CHIPS, columns)
    summed = jnp.where(core == 0, summed, jnp.roll(summed, columns // 2, axis=1))
    summed = jnp.pad(summed.astype(jnp.bfloat16), ((0, 0), (0, 512 - columns)))
    proj = exchange(summed.reshape(CHIPS, 4, 128), "gy", PLANE).reshape(CHIPS, 512)
    proj = proj[:, :columns].reshape(1, -1)
    attended_output = attend_cached_keys(proj, cache, cache_lengths).reshape(1, 96, 128)
    mine = exchange(jnp.broadcast_to(attended_output, (CHIPS, 96, 128)), "gy", PLANE)
    theirs = lax.ppermute(mine, "gy", SIBLING)
    return output_rows(core, mine, theirs, out_weight.T)


def solution(mesh):
    placed = (
        P("gy", "gx"),
        P("gx", "gy"),
        P(None, "gy"),
        P(("gx", "gy"), None, None, None),
        P(("gx", "gy")),
    )
    return jax.shard_map(
        on_device, mesh=mesh, in_specs=placed, out_specs=P("gx", "gy"), check_vma=False
    )
```

```python
import jax
import jax.numpy as jnp
from jax import lax
from jax.experimental import pallas as pl
from jax.experimental.pallas import tpu as pltpu
from jax.sharding import PartitionSpec as P

HEADS = 48
DH = 256

CHIPS = 32


def place(x_hi, z, core):
    return (x_hi * 8 + z) * 2 + core


def near_group(core, x_from, z_from):
    members = {}
    for dx in range(2):
        for dz in range(2):
            x_hi, z = (x_from + dx) % 4, (z_from + dz) % 8
            members[z % 2, x_hi % 2] = place(x_hi, z, core)
    return [members[key] for key in sorted(members)]


PLANE = [[place(chip // 8, chip % 8, core) for chip in range(CHIPS)] for core in range(2)]
NEAR = [
    near_group(core, 2 * a + core, 2 * b + core)
    for core in range(2)
    for a in range(2)
    for b in range(4)
]
FAR = [
    [
        (2 * pair + plane) * 64 + place(2 * a + e, 2 * b + w, core)
        for plane in range(2)
        for a in range(2)
        for b in range(4)
        for core in range(2)
    ]
    for pair in range(8)
    for e in range(2)
    for w in range(2)
]
OWNERS = [[8 * a + 4 * e + b for e in range(2) for a in range(2) for b in range(4)]]
SIBLING = [(i, i ^ 1) for i in range(2 * CHIPS)]
NEXT_PLANE = [(i, i ^ 1) for i in range(16)]


def rotate(vectors, token_position):
    half = vectors.shape[-1] // 2
    steps = jnp.arange(half).astype(jnp.float32)
    freqs = 10000.0 ** (-2.0 * steps / vectors.shape[-1])
    angle = token_position * freqs
    cosine = jnp.cos(angle)
    sine = jnp.sin(angle)
    first = vectors[..., :half]
    second = vectors[..., half:]
    return jnp.concatenate(
        [first * cosine - second * sine, second * cosine + first * sine], axis=-1
    )


def attend_cached_keys(proj, cache, cache_lengths):
    seq_here = proj.shape[0]
    width = HEADS * DH
    score_scale = DH ** (-0.5)
    token_position = cache_lengths.astype(jnp.float32)
    query_vector = proj[:, :width].astype(jnp.float32).reshape(seq_here, HEADS, DH)
    query_vector = rotate(query_vector, token_position[:, None, None]).astype(jnp.bfloat16)
    fresh_key = rotate(
        proj[:, width : width + DH].astype(jnp.float32), token_position[:, None]
    ).astype(jnp.bfloat16)
    fresh_value = proj[:, width + DH :]
    scores = (
        jnp.einsum("bpr,bar->bpa", query_vector, cache[:, 0], preferred_element_type=jnp.float32)
        * score_scale
    )
    valid = jnp.arange(cache.shape[2])[None, :] < cache_lengths[:, None]
    scores = jnp.where(valid[:, None, :], scores, -1e30)
    fresh = (
        jnp.einsum("shd,sd->sh", query_vector, fresh_key, preferred_element_type=jnp.float32)
        * score_scale
    )
    top = jnp.maximum(jnp.max(scores, axis=-1), fresh)
    expo = jnp.exp(scores - top[:, :, None])
    expo_fresh = jnp.exp(fresh - top)
    total = jnp.sum(expo, axis=-1) + expo_fresh
    softmax_weights = (expo / total[:, :, None]).astype(jnp.bfloat16)
    fresh_weight = (expo_fresh / total).astype(jnp.bfloat16)
    attended_output = jnp.einsum(
        "trj,tjp->trp", softmax_weights, cache[:, 1], preferred_element_type=jnp.float32
    )
    attended_output = (
        attended_output
        + fresh_weight.astype(jnp.float32)[:, :, None] * fresh_value.astype(jnp.float32)[:, None, :]
    )
    return attended_output.astype(jnp.bfloat16)


def exchange(blocks, axis, groups):
    return lax.all_to_all(
        blocks, axis, split_axis=0, concat_axis=0, axis_index_groups=groups, tiled=True
    )


CHUNKS = 6


def output_kernel(core_ref, mine_ref, theirs_ref, weights_ref, out_ref):
    tiles = mine_ref.shape[1] // CHUNKS
    depth = tiles * mine_ref.shape[2]
    total = jnp.zeros((weights_ref.shape[0], 2 * CHIPS), jnp.float32)
    for i in range(CHUNKS):
        here = slice(i * tiles, (i + 1) * tiles)
        rows = jnp.concatenate(
            [
                mine_ref[:, here, :].reshape(CHIPS, depth),
                theirs_ref[:, here, :].reshape(CHIPS, depth),
            ],
            axis=0,
        )
        total += lax.dot_general(
            weights_ref[:, i * depth : (i + 1) * depth],
            rows,
            (((1,), (1,)), ((), ())),
            preferred_element_type=jnp.float32,
        )
    place_of = lax.broadcasted_iota(jnp.int32, (2 * CHIPS, 2 * CHIPS), 0)
    row = lax.broadcasted_iota(jnp.int32, (2 * CHIPS, 2 * CHIPS), 1)
    order = ((place_of >> 1) == (row & (CHIPS - 1))) & (
        (place_of & 1) == ((row >> 5) ^ core_ref[0])
    )
    out_ref[...] = lax.dot_general(
        order.astype(jnp.float32).astype(jnp.bfloat16),
        total.astype(jnp.bfloat16),
        (((1,), (1,)), ((), ())),
        preferred_element_type=jnp.float32,
    ).astype(jnp.bfloat16)


def copy_kernel(core_ref, weights_ref, same_core_ref, copied_ref, sem):
    copy = pltpu.make_async_copy(weights_ref, copied_ref, sem)
    copy.start()
    same_core_ref[0] = core_ref[0]
    copy.wait()


def copy_weights(core, weights):
    smem = pl.BlockSpec(memory_space=pltpu.SMEM)
    hbm = pl.BlockSpec(memory_space=pltpu.HBM)
    return pl.pallas_call(
        copy_kernel,
        out_shape=(
            jax.ShapeDtypeStruct(core.shape, core.dtype),
            jax.ShapeDtypeStruct(weights.shape, weights.dtype),
        ),
        in_specs=[smem, hbm],
        out_specs=(smem, hbm),
        scratch_shapes=[pltpu.SemaphoreType.DMA],
        compiler_params=pltpu.CompilerParams(vmem_limit_bytes=54 * 2**20),
        cost_estimate=pl.CostEstimate(
            flops=0, bytes_accessed=4 * weights.size, transcendentals=0
        ),
    )(core, weights)


def hold_kernel(weights_ref, held_ref):
    pass


def hold(weights):
    vmem = pl.BlockSpec(memory_space=pltpu.VMEM)
    return pl.pallas_call(
        hold_kernel,
        out_shape=jax.ShapeDtypeStruct(weights.shape, weights.dtype),
        in_specs=[vmem],
        out_specs=vmem,
        input_output_aliases={0: 0},
        compiler_params=pltpu.CompilerParams(vmem_limit_bytes=46 * 2**20),
        cost_estimate=pl.CostEstimate(
            flops=0, bytes_accessed=2 * weights.size, transcendentals=0
        ),
    )(weights)


def output_rows(core, mine, theirs, weights):
    columns, depth = weights.shape
    vmem = pl.BlockSpec(memory_space=pltpu.VMEM)
    return pl.pallas_call(
        output_kernel,
        out_shape=jax.ShapeDtypeStruct((2 * CHIPS, columns), jnp.bfloat16),
        in_specs=[pl.BlockSpec(memory_space=pltpu.SMEM), vmem, vmem, vmem],
        out_specs=vmem,
        compiler_params=pltpu.CompilerParams(vmem_limit_bytes=32 * 2**20),
        cost_estimate=pl.CostEstimate(
            flops=4 * CHIPS * columns * depth,
            bytes_accessed=2 * columns * depth,
            transcendentals=0,
        ),
    )(core.astype(jnp.int32).reshape(1), mine, theirs, weights)


def on_device(tokens, qkv_weight, out_weight, cache, cache_lengths):
    core = lax.rem(lax.axis_index("gy"), 2)
    plane = lax.rem(lax.axis_index("gx"), 2)
    width = tokens.shape[1]
    split = tokens.reshape(4, 2, 2, width).transpose(1, 2, 0, 3)
    far = jnp.broadcast_to(split[:, None], (2, 8, 2, 4, width)).reshape(CHIPS, 4, width)
    far = exchange(far, ("gx", "gy"), FAR).reshape(2, 64, width)
    rows = jnp.concatenate([far[0], far[1]], axis=1)
    gathered = exchange(jnp.broadcast_to(rows[None], (4,) + rows.shape), "gy", NEAR)
    next_weight = lax.ppermute(qkv_weight, "gx", NEXT_PLANE)
    own_columns = jnp.concatenate(
        [
            jnp.where(plane == 0, qkv_weight, next_weight),
            jnp.where(plane == 0, next_weight, qkv_weight),
        ],
        axis=0,
    )
    weights = jnp.concatenate([own_columns, lax.ppermute(own_columns, "gy", SIBLING)], axis=1)
    partial_value = jnp.dot(
        gathered.reshape(256, 2 * width), weights, preferred_element_type=jnp.float32
    )
    columns = partial_value.shape[1]
    parts = lax.all_to_all(
        partial_value.reshape(2, 16, 8, columns),
        "gx",
        split_axis=1,
        concat_axis=1,
        axis_index_groups=OWNERS,
        tiled=True,
    )
    summed = jnp.sum(parts.reshape(2, 8, 2, 8, columns), axis=1)
    summed = summed.transpose(0, 2, 1, 3).reshape(CHIPS, columns)
    same_core, turned = copy_weights(core.astype(jnp.int32).reshape(1), out_weight.T)
    summed = jnp.where(same_core[0] == 0, summed, jnp.roll(summed, columns // 2, axis=1))
    summed = jnp.pad(summed.astype(jnp.bfloat16), ((0, 0), (0, 512 - columns)))
    proj = exchange(summed.reshape(CHIPS, 4, 128), "gy", PLANE).reshape(CHIPS, 512)
    proj = proj[:, :columns].reshape(1, -1)
    attended_output = attend_cached_keys(proj, cache, cache_lengths).reshape(1, 96, 128)
    mine = exchange(jnp.broadcast_to(attended_output, (CHIPS, 96, 128)), "gy", PLANE)
    theirs = lax.ppermute(mine, "gy", SIBLING)
    return output_rows(core, mine, theirs, hold(turned))


def solution(mesh):
    placed = (
        P("gy", "gx"),
        P("gx", "gy"),
        P(None, "gy"),
        P(("gx", "gy"), None, None, None),
        P(("gx", "gy")),
    )
    return jax.shard_map(
        on_device, mesh=mesh, in_specs=placed, out_specs=P("gx", "gy"), check_vma=False
    )
```

```python
import jax
import jax.numpy as jnp
from jax import lax
from jax.experimental import pallas as pl
from jax.experimental.pallas import tpu as pltpu
from jax.sharding import PartitionSpec as P

HEADS = 48
DH = 256

CHIPS = 32


def place(x_hi, z, core):
    return (x_hi * 8 + z) * 2 + core


def near_group(core, x_from, z_from):
    members = {}
    for dx in range(2):
        for dz in range(2):
            x_hi, z = (x_from + dx) % 4, (z_from + dz) % 8
            members[z % 2, x_hi % 2] = place(x_hi, z, core)
    return [members[key] for key in sorted(members)]


PLANE = [[place(chip // 8, chip % 8, core) for chip in range(CHIPS)] for core in range(2)]
NEAR = [
    near_group(core, 2 * a + core, 2 * b + core)
    for core in range(2)
    for a in range(2)
    for b in range(4)
]
FAR = [
    [
        (2 * pair + plane) * 64 + place(2 * a + e, 2 * b + w, core)
        for plane in range(2)
        for a in range(2)
        for b in range(4)
        for core in range(2)
    ]
    for pair in range(8)
    for e in range(2)
    for w in range(2)
]
OWNERS = [[8 * a + 4 * e + b for e in range(2) for a in range(2) for b in range(4)]]
SIBLING = [(i, i ^ 1) for i in range(2 * CHIPS)]
NEXT_PLANE = [(i, i ^ 1) for i in range(16)]


def rotate(vectors, token_position):
    half = vectors.shape[-1] // 2
    steps = jnp.arange(half).astype(jnp.float32)
    freqs = 10000.0 ** (-2.0 * steps / vectors.shape[-1])
    angle = token_position * freqs
    cosine = jnp.cos(angle)
    sine = jnp.sin(angle)
    first = vectors[..., :half]
    second = vectors[..., half:]
    return jnp.concatenate(
        [first * cosine - second * sine, second * cosine + first * sine], axis=-1
    )


def attend_cached_keys(proj, cache, cache_lengths):
    seq_here = proj.shape[0]
    width = HEADS * DH
    score_scale = DH ** (-0.5)
    token_position = cache_lengths.astype(jnp.float32)
    query_vector = proj[:, :width].astype(jnp.float32).reshape(seq_here, HEADS, DH)
    query_vector = rotate(query_vector, token_position[:, None, None]).astype(jnp.bfloat16)
    fresh_key = rotate(
        proj[:, width : width + DH].astype(jnp.float32), token_position[:, None]
    ).astype(jnp.bfloat16)
    fresh_value = proj[:, width + DH :]
    scores = (
        jnp.einsum("bpr,bar->bpa", query_vector, cache[:, 0], preferred_element_type=jnp.float32)
        * score_scale
    )
    valid = jnp.arange(cache.shape[2])[None, :] < cache_lengths[:, None]
    scores = jnp.where(valid[:, None, :], scores, -1e30)
    fresh = (
        jnp.einsum("shd,sd->sh", query_vector, fresh_key, preferred_element_type=jnp.float32)
        * score_scale
    )
    top = jnp.maximum(jnp.max(scores, axis=-1), fresh)
    expo = jnp.exp(scores - top[:, :, None])
    expo_fresh = jnp.exp(fresh - top)
    total = jnp.sum(expo, axis=-1) + expo_fresh
    softmax_weights = (expo / total[:, :, None]).astype(jnp.bfloat16)
    fresh_weight = (expo_fresh / total).astype(jnp.bfloat16)
    attended_output = jnp.einsum(
        "trj,tjp->trp", softmax_weights, cache[:, 1], preferred_element_type=jnp.float32
    )
    attended_output = (
        attended_output
        + fresh_weight.astype(jnp.float32)[:, :, None] * fresh_value.astype(jnp.float32)[:, None, :]
    )
    return attended_output.astype(jnp.bfloat16)


def exchange(blocks, axis, groups):
    return lax.all_to_all(
        blocks, axis, split_axis=0, concat_axis=0, axis_index_groups=groups, tiled=True
    )


CHUNKS = 6


def output_kernel(core_ref, mine_ref, theirs_ref, weights_ref, out_ref):
    tiles = mine_ref.shape[1] // CHUNKS
    depth = tiles * mine_ref.shape[2]
    total = jnp.zeros((weights_ref.shape[0], 2 * CHIPS), jnp.float32)
    for i in range(CHUNKS):
        here = slice(i * tiles, (i + 1) * tiles)
        rows = jnp.concatenate(
            [
                mine_ref[:, here, :].reshape(CHIPS, depth),
                theirs_ref[:, here, :].reshape(CHIPS, depth),
            ],
            axis=0,
        )
        total += lax.dot_general(
            weights_ref[:, i * depth : (i + 1) * depth],
            rows,
            (((1,), (1,)), ((), ())),
            preferred_element_type=jnp.float32,
        )
    place_of = lax.broadcasted_iota(jnp.int32, (2 * CHIPS, 2 * CHIPS), 0)
    row = lax.broadcasted_iota(jnp.int32, (2 * CHIPS, 2 * CHIPS), 1)
    order = ((place_of >> 1) == (row & (CHIPS - 1))) & (
        (place_of & 1) == ((row >> 5) ^ core_ref[0])
    )
    out_ref[...] = lax.dot_general(
        order.astype(jnp.float32).astype(jnp.bfloat16),
        total.astype(jnp.bfloat16),
        (((1,), (1,)), ((), ())),
        preferred_element_type=jnp.float32,
    ).astype(jnp.bfloat16)


def copy_kernel(core_ref, weights_ref, same_core_ref, copied_ref):
    same_core_ref[0] = core_ref[0]
    copied_ref[...] = weights_ref[...]


def copy_weights(core, weights):
    smem = pl.BlockSpec(memory_space=pltpu.SMEM)
    rows = pl.BlockSpec((32, weights.shape[1]), lambda step: (step, 0))
    return pl.pallas_call(
        copy_kernel,
        out_shape=(
            jax.ShapeDtypeStruct(core.shape, core.dtype),
            jax.ShapeDtypeStruct(weights.shape, weights.dtype),
        ),
        grid=(weights.shape[0] // 32,),
        in_specs=[smem, rows],
        out_specs=(smem, rows),
        compiler_params=pltpu.CompilerParams(vmem_limit_bytes=54 * 2**20),
        cost_estimate=pl.CostEstimate(
            flops=0, bytes_accessed=4 * weights.size, transcendentals=0
        ),
    )(core, weights)


def hold_kernel(weights_ref, held_ref):
    pass


def hold(weights):
    vmem = pl.BlockSpec(memory_space=pltpu.VMEM)
    return pl.pallas_call(
        hold_kernel,
        out_shape=jax.ShapeDtypeStruct(weights.shape, weights.dtype),
        in_specs=[vmem],
        out_specs=vmem,
        input_output_aliases={0: 0},
        compiler_params=pltpu.CompilerParams(vmem_limit_bytes=46 * 2**20),
        cost_estimate=pl.CostEstimate(
            flops=0, bytes_accessed=2 * weights.size, transcendentals=0
        ),
    )(weights)


def output_rows(core, mine, theirs, weights):
    columns, depth = weights.shape
    vmem = pl.BlockSpec(memory_space=pltpu.VMEM)
    return pl.pallas_call(
        output_kernel,
        out_shape=jax.ShapeDtypeStruct((2 * CHIPS, columns), jnp.bfloat16),
        in_specs=[pl.BlockSpec(memory_space=pltpu.SMEM), vmem, vmem, vmem],
        out_specs=vmem,
        compiler_params=pltpu.CompilerParams(vmem_limit_bytes=32 * 2**20),
        cost_estimate=pl.CostEstimate(
            flops=4 * CHIPS * columns * depth,
            bytes_accessed=2 * columns * depth,
            transcendentals=0,
        ),
    )(core.astype(jnp.int32).reshape(1), mine, theirs, weights)


def on_device(tokens, qkv_weight, out_weight, cache, cache_lengths):
    core = lax.rem(lax.axis_index("gy"), 2)
    plane = lax.rem(lax.axis_index("gx"), 2)
    width = tokens.shape[1]
    split = tokens.reshape(4, 2, 2, width).transpose(1, 2, 0, 3)
    far = jnp.broadcast_to(split[:, None], (2, 8, 2, 4, width)).reshape(CHIPS, 4, width)
    far = exchange(far, ("gx", "gy"), FAR).reshape(2, 64, width)
    rows = jnp.concatenate([far[0], far[1]], axis=1)
    gathered = exchange(jnp.broadcast_to(rows[None], (4,) + rows.shape), "gy", NEAR)
    next_weight = lax.ppermute(qkv_weight, "gx", NEXT_PLANE)
    own_columns = jnp.concatenate(
        [
            jnp.where(plane == 0, qkv_weight, next_weight),
            jnp.where(plane == 0, next_weight, qkv_weight),
        ],
        axis=0,
    )
    weights = jnp.concatenate([own_columns, lax.ppermute(own_columns, "gy", SIBLING)], axis=1)
    partial_value = jnp.dot(
        gathered.reshape(256, 2 * width), weights, preferred_element_type=jnp.float32
    )
    columns = partial_value.shape[1]
    parts = lax.all_to_all(
        partial_value.reshape(2, 16, 8, columns),
        "gx",
        split_axis=1,
        concat_axis=1,
        axis_index_groups=OWNERS,
        tiled=True,
    )
    summed = jnp.sum(parts.reshape(2, 8, 2, 8, columns), axis=1)
    summed = summed.transpose(0, 2, 1, 3).reshape(CHIPS, columns)
    same_core, turned = copy_weights(core.astype(jnp.int32).reshape(1), out_weight.T)
    summed = jnp.where(same_core[0] == 0, summed, jnp.roll(summed, columns // 2, axis=1))
    summed = jnp.pad(summed.astype(jnp.bfloat16), ((0, 0), (0, 512 - columns)))
    proj = exchange(summed.reshape(CHIPS, 4, 128), "gy", PLANE).reshape(CHIPS, 512)
    proj = proj[:, :columns].reshape(1, -1)
    attended_output = attend_cached_keys(proj, cache, cache_lengths).reshape(1, 96, 128)
    mine = exchange(jnp.broadcast_to(attended_output, (CHIPS, 96, 128)), "gy", PLANE)
    theirs = lax.ppermute(mine, "gy", SIBLING)
    return output_rows(core, mine, theirs, hold(turned))


def solution(mesh):
    placed = (
        P("gy", "gx"),
        P("gx", "gy"),
        P(None, "gy"),
        P(("gx", "gy"), None, None, None),
        P(("gx", "gy")),
    )
    return jax.shard_map(
        on_device, mesh=mesh, in_specs=placed, out_specs=P("gx", "gy"), check_vma=False
    )
```

```python
import jax
import jax.numpy as jnp
from jax import lax
from jax.experimental import pallas as pl
from jax.experimental.pallas import tpu as pltpu
from jax.sharding import PartitionSpec as P

HEADS = 48
DH = 256

CHIPS = 32


def place(x_hi, z, core):
    return (x_hi * 8 + z) * 2 + core


def near_group(core, x_from, z_from):
    members = {}
    for dx in range(2):
        for dz in range(2):
            x_hi, z = (x_from + dx) % 4, (z_from + dz) % 8
            members[z % 2, x_hi % 2] = place(x_hi, z, core)
    return [members[key] for key in sorted(members)]


PLANE = [[place(chip // 8, chip % 8, core) for chip in range(CHIPS)] for core in range(2)]
NEAR = [
    near_group(core, 2 * a + core, 2 * b + core)
    for core in range(2)
    for a in range(2)
    for b in range(4)
]
FAR = [
    [
        (2 * pair + plane) * 64 + place(2 * a + e, 2 * b + w, core)
        for a in range(2)
        for b in range(4)
        for core in range(2)
        for plane in range(2)
    ]
    for pair in range(8)
    for e in range(2)
    for w in range(2)
]
OWNERS = [[8 * a + 4 * e + b for e in range(2) for a in range(2) for b in range(4)]]
SIBLING = [(i, i ^ 1) for i in range(2 * CHIPS)]
NEXT_PLANE = [(i, i ^ 1) for i in range(16)]


def rotate(vectors, token_position):
    half = vectors.shape[-1] // 2
    steps = jnp.arange(half).astype(jnp.float32)
    freqs = 10000.0 ** (-2.0 * steps / vectors.shape[-1])
    angle = token_position * freqs
    cosine = jnp.cos(angle)
    sine = jnp.sin(angle)
    first = vectors[..., :half]
    second = vectors[..., half:]
    return jnp.concatenate(
        [first * cosine - second * sine, second * cosine + first * sine], axis=-1
    )


def attend_cached_keys(proj, cache, cache_lengths):
    seq_here = proj.shape[0]
    width = HEADS * DH
    score_scale = DH ** (-0.5)
    token_position = cache_lengths.astype(jnp.float32)
    query_vector = proj[:, :width].astype(jnp.float32).reshape(seq_here, HEADS, DH)
    query_vector = rotate(query_vector, token_position[:, None, None]).astype(jnp.bfloat16)
    fresh_key = rotate(
        proj[:, width : width + DH].astype(jnp.float32), token_position[:, None]
    ).astype(jnp.bfloat16)
    fresh_value = proj[:, width + DH :]
    scores = (
        jnp.einsum("bpr,bar->bpa", query_vector, cache[:, 0], preferred_element_type=jnp.float32)
        * score_scale
    )
    valid = jnp.arange(cache.shape[2])[None, :] < cache_lengths[:, None]
    scores = jnp.where(valid[:, None, :], scores, -1e30)
    fresh = (
        jnp.einsum("shd,sd->sh", query_vector, fresh_key, preferred_element_type=jnp.float32)
        * score_scale
    )
    top = jnp.maximum(jnp.max(scores, axis=-1), fresh)
    expo = jnp.exp(scores - top[:, :, None])
    expo_fresh = jnp.exp(fresh - top)
    total = jnp.sum(expo, axis=-1) + expo_fresh
    softmax_weights = (expo / total[:, :, None]).astype(jnp.bfloat16)
    fresh_weight = (expo_fresh / total).astype(jnp.bfloat16)
    attended_output = jnp.einsum(
        "trj,tjp->trp", softmax_weights, cache[:, 1], preferred_element_type=jnp.float32
    )
    attended_output = (
        attended_output
        + fresh_weight.astype(jnp.float32)[:, :, None] * fresh_value.astype(jnp.float32)[:, None, :]
    )
    return attended_output.astype(jnp.bfloat16)


def exchange(blocks, axis, groups):
    return lax.all_to_all(
        blocks, axis, split_axis=0, concat_axis=0, axis_index_groups=groups, tiled=True
    )


CHUNKS = 6


def output_kernel(core_ref, mine_ref, theirs_ref, weights_ref, out_ref):
    tiles = mine_ref.shape[1] // CHUNKS
    depth = tiles * mine_ref.shape[2]
    total = jnp.zeros((weights_ref.shape[0], 2 * CHIPS), jnp.float32)
    for i in range(CHUNKS):
        here = slice(i * tiles, (i + 1) * tiles)
        rows = jnp.concatenate(
            [
                mine_ref[:, here, :].reshape(CHIPS, depth),
                theirs_ref[:, here, :].reshape(CHIPS, depth),
            ],
            axis=0,
        )
        total += lax.dot_general(
            weights_ref[:, i * depth : (i + 1) * depth],
            rows,
            (((1,), (1,)), ((), ())),
            preferred_element_type=jnp.float32,
        )
    place_of = lax.broadcasted_iota(jnp.int32, (2 * CHIPS, 2 * CHIPS), 0)
    row = lax.broadcasted_iota(jnp.int32, (2 * CHIPS, 2 * CHIPS), 1)
    order = ((place_of >> 1) == (row & (CHIPS - 1))) & (
        (place_of & 1) == ((row >> 5) ^ core_ref[0])
    )
    out_ref[...] = lax.dot_general(
        order.astype(jnp.float32).astype(jnp.bfloat16),
        total.astype(jnp.bfloat16),
        (((1,), (1,)), ((), ())),
        preferred_element_type=jnp.float32,
    ).astype(jnp.bfloat16)


def copy_kernel(core_ref, weights_ref, same_core_ref, copied_ref):
    same_core_ref[0] = core_ref[0]
    copied_ref[...] = weights_ref[...]


def copy_weights(core, weights):
    smem = pl.BlockSpec(memory_space=pltpu.SMEM)
    rows = pl.BlockSpec((32, weights.shape[1]), lambda step: (step, 0))
    return pl.pallas_call(
        copy_kernel,
        out_shape=(
            jax.ShapeDtypeStruct(core.shape, core.dtype),
            jax.ShapeDtypeStruct(weights.shape, weights.dtype),
        ),
        grid=(weights.shape[0] // 32,),
        in_specs=[smem, rows],
        out_specs=(smem, rows),
        compiler_params=pltpu.CompilerParams(vmem_limit_bytes=54 * 2**20),
        cost_estimate=pl.CostEstimate(
            flops=0, bytes_accessed=4 * weights.size, transcendentals=0
        ),
    )(core, weights)


def hold_kernel(weights_ref, held_ref):
    pass


def hold(weights):
    vmem = pl.BlockSpec(memory_space=pltpu.VMEM)
    return pl.pallas_call(
        hold_kernel,
        out_shape=jax.ShapeDtypeStruct(weights.shape, weights.dtype),
        in_specs=[vmem],
        out_specs=vmem,
        input_output_aliases={0: 0},
        compiler_params=pltpu.CompilerParams(vmem_limit_bytes=46 * 2**20),
        cost_estimate=pl.CostEstimate(
            flops=0, bytes_accessed=2 * weights.size, transcendentals=0
        ),
    )(weights)


def output_rows(core, mine, theirs, weights):
    columns, depth = weights.shape
    vmem = pl.BlockSpec(memory_space=pltpu.VMEM)
    return pl.pallas_call(
        output_kernel,
        out_shape=jax.ShapeDtypeStruct((2 * CHIPS, columns), jnp.bfloat16),
        in_specs=[pl.BlockSpec(memory_space=pltpu.SMEM), vmem, vmem, vmem],
        out_specs=vmem,
        compiler_params=pltpu.CompilerParams(vmem_limit_bytes=32 * 2**20),
        cost_estimate=pl.CostEstimate(
            flops=4 * CHIPS * columns * depth,
            bytes_accessed=2 * columns * depth,
            transcendentals=0,
        ),
    )(core.astype(jnp.int32).reshape(1), mine, theirs, weights)


def on_device(tokens, qkv_weight, out_weight, cache, cache_lengths):
    core = lax.rem(lax.axis_index("gy"), 2)
    plane = lax.rem(lax.axis_index("gx"), 2)
    width = tokens.shape[1]
    split = tokens.reshape(4, 2, 2, width).transpose(2, 1, 0, 3)
    far = jnp.broadcast_to(split[None], (8, 2, 2, 4, width)).reshape(CHIPS, 4, width)
    far = exchange(far, ("gx", "gy"), FAR).reshape(16, 2, 4, width)
    rows = jnp.concatenate(
        [far[:, 0].reshape(64, width), far[:, 1].reshape(64, width)], axis=1
    )
    gathered = exchange(jnp.broadcast_to(rows[None], (4,) + rows.shape), "gy", NEAR)
    next_weight = lax.ppermute(qkv_weight, "gx", NEXT_PLANE)
    own_columns = jnp.concatenate(
        [
            jnp.where(plane == 0, qkv_weight, next_weight),
            jnp.where(plane == 0, next_weight, qkv_weight),
        ],
        axis=0,
    )
    weights = jnp.concatenate([own_columns, lax.ppermute(own_columns, "gy", SIBLING)], axis=1)
    partial_value = jnp.dot(
        gathered.reshape(256, 2 * width), weights, preferred_element_type=jnp.float32
    )
    columns = partial_value.shape[1]
    parts = lax.all_to_all(
        partial_value.reshape(2, 16, 8, columns),
        "gx",
        split_axis=1,
        concat_axis=1,
        axis_index_groups=OWNERS,
        tiled=True,
    )
    summed = jnp.sum(parts.reshape(2, 8, 2, 8, columns), axis=1)
    summed = summed.transpose(0, 2, 1, 3).reshape(CHIPS, columns)
    same_core, turned = copy_weights(core.astype(jnp.int32).reshape(1), out_weight.T)
    summed = jnp.where(same_core[0] == 0, summed, jnp.roll(summed, columns // 2, axis=1))
    summed = jnp.pad(summed.astype(jnp.bfloat16), ((0, 0), (0, 512 - columns)))
    proj = exchange(summed.reshape(CHIPS, 4, 128), "gy", PLANE).reshape(CHIPS, 512)
    proj = proj[:, :columns].reshape(1, -1)
    attended_output = attend_cached_keys(proj, cache, cache_lengths).reshape(1, 96, 128)
    mine = exchange(jnp.broadcast_to(attended_output, (CHIPS, 96, 128)), "gy", PLANE)
    theirs = lax.ppermute(mine, "gy", SIBLING)
    return output_rows(core, mine, theirs, hold(turned))


def solution(mesh):
    placed = (
        P("gy", "gx"),
        P("gx", "gy"),
        P(None, "gy"),
        P(("gx", "gy"), None, None, None),
        P(("gx", "gy")),
    )
    return jax.shard_map(
        on_device, mesh=mesh, in_specs=placed, out_specs=P("gx", "gy"), check_vma=False
    )
```

```python
import jax
import jax.numpy as jnp
from jax import lax
from jax.experimental import pallas as pl
from jax.experimental.pallas import tpu as pltpu
from jax.sharding import PartitionSpec as P

HEADS = 48
DH = 256

CHIPS = 32


def place(x_hi, z, core):
    return (x_hi * 8 + z) * 2 + core


def near_group(core, x_from, z_from):
    members = {}
    for dx in range(2):
        for dz in range(2):
            x_hi, z = (x_from + dx) % 4, (z_from + dz) % 8
            members[z % 2, x_hi % 2] = place(x_hi, z, core)
    return [members[key] for key in sorted(members)]


PLANE = [[place(chip // 8, chip % 8, core) for chip in range(CHIPS)] for core in range(2)]
NEAR = [
    near_group(core, 2 * a + core, 2 * b + core)
    for core in range(2)
    for a in range(2)
    for b in range(4)
]
FAR = [
    [
        (2 * pair + plane) * 64 + place(2 * a + e, 2 * b + w, core)
        for a in range(2)
        for b in range(4)
        for core in range(2)
        for plane in range(2)
    ]
    for pair in range(8)
    for e in range(2)
    for w in range(2)
]
OWNERS = [[8 * a + 4 * e + b for e in range(2) for a in range(2) for b in range(4)]]
SIBLING = [(i, i ^ 1) for i in range(2 * CHIPS)]
NEXT_PLANE = [(i, i ^ 1) for i in range(16)]


def rotate(vectors, token_position):
    half = vectors.shape[-1] // 2
    steps = jnp.arange(half).astype(jnp.float32)
    freqs = 10000.0 ** (-2.0 * steps / vectors.shape[-1])
    angle = token_position * freqs
    cosine = jnp.cos(angle)
    sine = jnp.sin(angle)
    first = vectors[..., :half]
    second = vectors[..., half:]
    return jnp.concatenate(
        [first * cosine - second * sine, second * cosine + first * sine], axis=-1
    )


def attend_cached_keys(proj, cache, cache_lengths):
    seq_here = proj.shape[0]
    width = HEADS * DH
    score_scale = DH ** (-0.5)
    token_position = cache_lengths.astype(jnp.float32)
    query_vector = proj[:, :width].astype(jnp.float32).reshape(seq_here, HEADS, DH)
    query_vector = rotate(query_vector, token_position[:, None, None]).astype(jnp.bfloat16)
    fresh_key = rotate(
        proj[:, width : width + DH].astype(jnp.float32), token_position[:, None]
    ).astype(jnp.bfloat16)
    fresh_value = proj[:, width + DH :]
    scores = (
        jnp.einsum("bpr,bar->bpa", query_vector, cache[:, 0], preferred_element_type=jnp.float32)
        * score_scale
    )
    valid = jnp.arange(cache.shape[2])[None, :] < cache_lengths[:, None]
    scores = jnp.where(valid[:, None, :], scores, -1e30)
    fresh = (
        jnp.einsum("shd,sd->sh", query_vector, fresh_key, preferred_element_type=jnp.float32)
        * score_scale
    )
    top = jnp.maximum(jnp.max(scores, axis=-1), fresh)
    expo = jnp.exp(scores - top[:, :, None])
    expo_fresh = jnp.exp(fresh - top)
    total = jnp.sum(expo, axis=-1) + expo_fresh
    softmax_weights = (expo / total[:, :, None]).astype(jnp.bfloat16)
    fresh_weight = (expo_fresh / total).astype(jnp.bfloat16)
    attended_output = jnp.einsum(
        "trj,tjp->trp", softmax_weights, cache[:, 1], preferred_element_type=jnp.float32
    )
    attended_output = (
        attended_output
        + fresh_weight.astype(jnp.float32)[:, :, None] * fresh_value.astype(jnp.float32)[:, None, :]
    )
    return attended_output.astype(jnp.bfloat16)


def exchange(blocks, axis, groups):
    return lax.all_to_all(
        blocks, axis, split_axis=0, concat_axis=0, axis_index_groups=groups, tiled=True
    )


CHUNKS = 6


def output_kernel(core_ref, mine_ref, theirs_ref, lower_ref, upper_ref, out_ref):
    tiles = mine_ref.shape[1] // CHUNKS
    depth = tiles * mine_ref.shape[2]
    total = jnp.zeros((lower_ref.shape[0], 2 * CHIPS), jnp.float32)
    for i in range(CHUNKS):
        here = slice(i * tiles, (i + 1) * tiles)
        rows = jnp.concatenate(
            [
                mine_ref[:, here, :].reshape(CHIPS, depth),
                theirs_ref[:, here, :].reshape(CHIPS, depth),
            ],
            axis=0,
        )
        half, k = (lower_ref, i) if i < CHUNKS // 2 else (upper_ref, i - CHUNKS // 2)
        total += lax.dot_general(
            half[:, k * depth : (k + 1) * depth],
            rows,
            (((1,), (1,)), ((), ())),
            preferred_element_type=jnp.float32,
        )
    place_of = lax.broadcasted_iota(jnp.int32, (2 * CHIPS, 2 * CHIPS), 0)
    row = lax.broadcasted_iota(jnp.int32, (2 * CHIPS, 2 * CHIPS), 1)
    order = ((place_of >> 1) == (row & (CHIPS - 1))) & (
        (place_of & 1) == ((row >> 5) ^ core_ref[0])
    )
    out_ref[...] = lax.dot_general(
        order.astype(jnp.float32).astype(jnp.bfloat16),
        total.astype(jnp.bfloat16),
        (((1,), (1,)), ((), ())),
        preferred_element_type=jnp.float32,
    ).astype(jnp.bfloat16)


def copy_kernel(core_ref, weights_ref, same_core_ref, lower_ref, upper_ref):
    half = lower_ref.shape[1]
    same_core_ref[0] = core_ref[0]
    lower_ref[...] = weights_ref[:, :half]
    upper_ref[...] = weights_ref[:, half:]


def copy_weights(core, weights):
    smem = pl.BlockSpec(memory_space=pltpu.SMEM)
    rows = pl.BlockSpec((32, weights.shape[1]), lambda step: (step, 0))
    half_rows = pl.BlockSpec((32, weights.shape[1] // 2), lambda step: (step, 0))
    half = jax.ShapeDtypeStruct((weights.shape[0], weights.shape[1] // 2), weights.dtype)
    return pl.pallas_call(
        copy_kernel,
        out_shape=(
            jax.ShapeDtypeStruct(core.shape, core.dtype),
            half,
            half,
        ),
        grid=(weights.shape[0] // 32,),
        in_specs=[smem, rows],
        out_specs=(smem, half_rows, half_rows),
        compiler_params=pltpu.CompilerParams(vmem_limit_bytes=54 * 2**20),
        cost_estimate=pl.CostEstimate(
            flops=0, bytes_accessed=4 * weights.size, transcendentals=0
        ),
    )(core, weights)


def hold_kernel(weights_ref, held_ref):
    pass


def hold(weights):
    vmem = pl.BlockSpec(memory_space=pltpu.VMEM)
    return pl.pallas_call(
        hold_kernel,
        out_shape=jax.ShapeDtypeStruct(weights.shape, weights.dtype),
        in_specs=[vmem],
        out_specs=vmem,
        input_output_aliases={0: 0},
        compiler_params=pltpu.CompilerParams(vmem_limit_bytes=46 * 2**20),
        cost_estimate=pl.CostEstimate(
            flops=0, bytes_accessed=2 * weights.size, transcendentals=0
        ),
    )(weights)


def output_rows(core, mine, theirs, lower, upper):
    columns, depth = lower.shape[0], 2 * lower.shape[1]
    vmem = pl.BlockSpec(memory_space=pltpu.VMEM)
    return pl.pallas_call(
        output_kernel,
        out_shape=jax.ShapeDtypeStruct((2 * CHIPS, columns), jnp.bfloat16),
        in_specs=[pl.BlockSpec(memory_space=pltpu.SMEM), vmem, vmem, vmem, vmem],
        out_specs=vmem,
        compiler_params=pltpu.CompilerParams(vmem_limit_bytes=32 * 2**20),
        cost_estimate=pl.CostEstimate(
            flops=4 * CHIPS * columns * depth,
            bytes_accessed=2 * columns * depth,
            transcendentals=0,
        ),
    )(core.astype(jnp.int32).reshape(1), mine, theirs, lower, upper)


def on_device(tokens, qkv_weight, out_weight, cache, cache_lengths):
    core = lax.rem(lax.axis_index("gy"), 2)
    plane = lax.rem(lax.axis_index("gx"), 2)
    width = tokens.shape[1]
    split = tokens.reshape(4, 2, 2, width).transpose(2, 1, 0, 3)
    far = jnp.broadcast_to(split[None], (8, 2, 2, 4, width)).reshape(CHIPS, 4, width)
    far = exchange(far, ("gx", "gy"), FAR).reshape(16, 2, 4, width)
    rows = jnp.concatenate(
        [far[:, 0].reshape(64, width), far[:, 1].reshape(64, width)], axis=1
    )
    gathered = exchange(jnp.broadcast_to(rows[None], (4,) + rows.shape), "gy", NEAR)
    next_weight = lax.ppermute(qkv_weight, "gx", NEXT_PLANE)
    own_columns = jnp.concatenate(
        [
            jnp.where(plane == 0, qkv_weight, next_weight),
            jnp.where(plane == 0, next_weight, qkv_weight),
        ],
        axis=0,
    )
    weights = jnp.concatenate([own_columns, lax.ppermute(own_columns, "gy", SIBLING)], axis=1)
    partial_value = jnp.dot(
        gathered.reshape(256, 2 * width), weights, preferred_element_type=jnp.float32
    )
    columns = partial_value.shape[1]
    parts = lax.all_to_all(
        partial_value.reshape(2, 16, 8, columns),
        "gx",
        split_axis=1,
        concat_axis=1,
        axis_index_groups=OWNERS,
        tiled=True,
    )
    summed = jnp.sum(parts.reshape(2, 8, 2, 8, columns), axis=1)
    summed = summed.transpose(0, 2, 1, 3).reshape(CHIPS, columns)
    same_core, lower, upper = copy_weights(core.astype(jnp.int32).reshape(1), out_weight.T)
    summed = jnp.where(same_core[0] == 0, summed, jnp.roll(summed, columns // 2, axis=1))
    summed = jnp.pad(summed.astype(jnp.bfloat16), ((0, 0), (0, 512 - columns)))
    proj = exchange(summed.reshape(CHIPS, 4, 128), "gy", PLANE).reshape(CHIPS, 512)
    proj = proj[:, :columns].reshape(1, -1)
    attended_output = attend_cached_keys(proj, cache, cache_lengths).reshape(1, 96, 128)
    mine = exchange(jnp.broadcast_to(attended_output, (CHIPS, 96, 128)), "gy", PLANE)
    theirs = lax.ppermute(mine, "gy", SIBLING)
    return output_rows(core, mine, theirs, lower, hold(upper))


def solution(mesh):
    placed = (
        P("gy", "gx"),
        P("gx", "gy"),
        P(None, "gy"),
        P(("gx", "gy"), None, None, None),
        P(("gx", "gy")),
    )
    return jax.shard_map(
        on_device, mesh=mesh, in_specs=placed, out_specs=P("gx", "gy"), check_vma=False
    )
```
